32 devices in a mesh: feeder: 16 (over z, y, core), factor: 2 (over x).
Axes of the slice: x: 2, y: 2, z: 4, core: 2. Of those that a mesh axis runs over, the one named last changes fastest.
Arguments:
- sensitivity: bfloat16 [16, 2048, 2048], P('feeder'), may hold values from -0.015625 to 0.015625
- headroom: float32 [16, 8, 2048], P('feeder'), may hold values from 0 to 3
- ev_power: float32 [16, 8, 256], P('feeder'), may hold values from 0.5 to 4
- ev_node: int32 [16, 8, 256], P('feeder'), may hold values from 0 to 2047
- region_map: int32 [16, 256], P('feeder'), may hold values from 0 to 255
- loadings: float32 [256, 8, 512], P('feeder', None, 'factor'), may hold values from -8 to 8
Outputs:
- margin: float32 [16, 8, 2048], P('feeder')
- new_loadings: float32 [256, 8, 512], P('feeder', None, 'factor')
The draws below stay inside these ranges and needn't reach their ends.
All inputs are finite; a program needn't handle non-finite values.
Results may differ from the reference program's by a relative error of at most 0.0031.
Values may be sent and summed in bfloat16 or wider, within the bound.
A program may use at most 64 MiB of HBM per device.

```python
import math
import jax
import jax.numpy as jnp
from jax import lax

NODES = 2048
RANK = 512
INTERVALS = 8
EVS = 256
FEEDERS = 16
REGIONS = 256


def draw_loadings(key, part):
    first_key = jax.random.fold_in(key, 11)
    column = jnp.arange(RANK, dtype=jnp.float32) / float(max(RANK - 1, 1))
    values = jax.random.normal(first_key, (REGIONS, INTERVALS, RANK), jnp.float32)
    values = values * (3.0 ** column / 1.9)[None, None, :]
    return jnp.clip(values, -8.0, 8.0).astype(jnp.float32)


def with_ends(values, own_key, low, high):
    index_at = [jax.random.randint(jax.random.fold_in(own_key, axis), (), 0, length) for axis, length in enumerate(values.shape)]
    longest = values.shape.index(max(values.shape))
    next_to = index_at[:longest] + [(index_at[longest] + 1) % values.shape[longest]] + index_at[longest + 1:]
    return values.at[tuple(index_at)].set(low).at[tuple(next_to)].set(high)


def block_scale(stream_key, shape, pieces, least, top_value):
    level = 1.0
    for axis_at, blocks in pieces:
        heights = jax.random.uniform(jax.random.fold_in(jax.random.fold_in(stream_key, 6), axis_at), (blocks,), jnp.float32, least / len(pieces), top_value / len(pieces))
        level = level * jnp.repeat(jnp.exp(heights), shape[axis_at] // blocks).reshape((-1,) + (1,) * (len(shape) - 1 - axis_at))
    return level


def gaussian(key, extent, scale, limit, cuts=(), kind=jnp.bfloat16):
    drawn = jax.random.normal(key, extent, jnp.float32) * scale
    if len(cuts) > 0:
        drawn = block_scale(key, extent, cuts, -0.22, 0.18) * drawn
    return jnp.clip(drawn, min=-limit, max=limit).astype(kind)


def setup_inputs(seed: int = 0) -> dict:
    seeds = jax.random.split(jax.random.key(seed), 7)
    sensitivity = gaussian(seeds[0], (FEEDERS, NODES, NODES), (EVS * RANK) ** -0.5, 0.015625, ((0, 16),))
    headroom = jnp.clip(3.0 * jax.random.uniform(seeds[1], (FEEDERS, INTERVALS, NODES), jnp.float32) ** block_scale(seeds[1], (FEEDERS, INTERVALS, NODES), ((0, 16),), -0.2, 0.2), 0.0, 3.0)
    ev_power = jnp.clip(jnp.exp(math.log(4.0) - 2.0794415 * jax.random.uniform(seeds[2], (FEEDERS, INTERVALS, EVS), jnp.float32) ** block_scale(seeds[2], (FEEDERS, INTERVALS, EVS), ((0, 16),), -0.2, 0.2)), 0.5, 4.0)
    ev_node = with_ends(jax.random.randint(seeds[3], (FEEDERS, INTERVALS, EVS), 0, NODES), jax.random.fold_in(seeds[3], 1), 0, NODES - 1).astype(jnp.int32)
    region_map = with_ends(jax.random.randint(seeds[4], (FEEDERS, EVS), 0, REGIONS), jax.random.fold_in(seeds[4], 1), 0, REGIONS - 1).astype(jnp.int32)
    loadings = draw_loadings(jax.random.fold_in(seeds[6], 71), 0)
    return {"sensitivity": sensitivity, "headroom": headroom, "ev_power": ev_power, "ev_node": ev_node, "region_map": region_map, "loadings": loadings}


quantile = 1.645
epsilon = 1e-06
step_size = 16.0

def reference(sensitivity, headroom, ev_power, ev_node, region_map, loadings):
    rounded = loadings.astype(jnp.bfloat16)

    def per_feeder(grad_total, inputs):
        sens_block, room, power, nodes, regions = inputs
        looked = rounded[regions].astype(jnp.float32)
        volts_list = []
        rows_list = []
        variance_list = []
        for interval in range(INTERVALS):
            weighted = (power[interval][:, None] * looked[:, interval, :]).astype(jnp.bfloat16)
            sens_rows = sens_block[nodes[interval]]
            factor_volts = jnp.dot(weighted.T, sens_rows, preferred_element_type=jnp.float32)
            volts_list.append(factor_volts)
            rows_list.append(sens_rows)
            variance_list.append(lax.optimization_barrier(jnp.sum(factor_volts * factor_volts, axis=0)))
        variance = jnp.stack(variance_list, axis=0)
        deviation = jnp.sqrt(variance + epsilon)
        margin = room - quantile * deviation
        violation = jnp.maximum(-margin, 0.0)
        var_grad = quantile * violation / deviation
        grads = []
        for interval in range(INTERVALS):
            volt_grad = (2.0 * var_grad[interval][None, :] * volts_list[interval]).astype(jnp.bfloat16)
            weight_grad = jnp.dot(rows_list[interval], volt_grad.T, preferred_element_type=jnp.float32)
            grads.append(power[interval][:, None] * weight_grad)
        load_grad = jnp.stack(grads, axis=1)
        grad_total = grad_total + jax.ops.segment_sum(load_grad, regions, num_segments=REGIONS)
        return (grad_total, margin)
    initial = jnp.zeros((REGIONS, INTERVALS, RANK), jnp.float32)
    grad_total, margins = lax.scan(per_feeder, initial, (sensitivity, headroom, ev_power, ev_node, region_map))
    return (margins, loadings - step_size * grad_total)
```

```python
import functools

import jax
import jax.numpy as jnp
from jax import lax
from jax.experimental import pallas as pl
from jax.experimental.pallas import tpu as pltpu
from jax.sharding import PartitionSpec as P

quantile = 1.645
epsilon = 1e-06
step_size = 16.0

CORES = 2
GROUPS = 2
MESH = pl.DeviceIdType.MESH
ROWS_BY_ROWS = (((1,), (1,)), ((), ()))
COLS_BY_COLS = (((0,), (0,)), ((), ()))


def kernel(
    peers, slices, tile,
    sens_hbm, headroom_ref, power_ref, node_ref, region_ref, load_ref,
    margin_ref, new_ref,
    sens, picks, rows, volts, match, gathered, coef, var_out, var_in,
    grad, grad_in, grad_out, grad_recv,
    sens_sem, ag_send, ag_recv, agc_send, agc_recv, var_send, var_recv,
    rsc_send, rsc_recv, rs_send, rs_recv,
):
    hours, ev_count, nodes = rows.shape
    local = load_ref.shape[0]
    half = peers * local
    span = hours // GROUPS
    tiles = nodes // tile
    feeder = lax.axis_index("feeder")
    factor = lax.axis_index("factor")
    core = lax.rem(feeder, CORES)
    place = lax.div(feeder, CORES)
    sibling = (place * CORES + (1 - core), factor)

    def peer(step):
        return lax.rem(place + step, peers)

    def peer_id(step):
        return (peer(step) * CORES + core, factor)

    def slice_id(step):
        return (feeder, lax.rem(factor + step, slices))

    def sens_copy(t):
        cols = pl.ds(t * tile, tile)
        return pltpu.make_async_copy(
            sens_hbm.at[0, :, cols], sens.at[:, cols], sens_sem.at[t]
        )

    for t in range(tiles):
        sens_copy(t).start()

    barrier = pltpu.get_barrier_semaphore()
    for step in range(1, peers):
        pl.semaphore_signal(barrier, inc=1, device_id=peer_id(step), device_id_type=MESH)
    for step in range(1, slices):
        pl.semaphore_signal(barrier, inc=1, device_id=slice_id(step), device_id_type=MESH)
    pl.semaphore_signal(barrier, inc=1, device_id=sibling, device_id_type=MESH)

    own = pl.ds(pl.multiple_of(place * local, local), local)
    for hour in range(hours):
        gathered[hour, core, own, :] = load_ref[:, hour, :].astype(jnp.bfloat16)

    pl.semaphore_wait(barrier, peers + slices - 1)

    def remote(src, dst, send, recv, device):
        return pltpu.make_async_remote_copy(
            src_ref=src, dst_ref=dst, send_sem=send, recv_sem=recv,
            device_id=device, device_id_type=MESH,
        )

    def ag_copy(g, step):
        block = gathered.at[pl.ds(g * span, span), core, own, :]
        return remote(block, block, ag_send.at[g, step], ag_recv.at[g, step], peer_id(step))

    def agc_copy(g):
        block = gathered.at[pl.ds(g * span, span), core]
        return remote(block, block, agc_send.at[g], agc_recv.at[g], sibling)

    def var_copy(g, step):
        return remote(
            var_out.at[g], var_in.at[g, step], var_send.at[g, step], var_recv.at[g, step],
            slice_id(step),
        )

    def rsc_copy(hour):
        return remote(
            grad.at[hour, 1 - core], grad_in.at[hour], rsc_send.at[hour], rsc_recv.at[hour],
            sibling,
        )

    def rs_copy(hour, step):
        block = pl.ds(pl.multiple_of(peer(step) * local, local), local)
        return remote(
            grad_out.at[hour, block, :], grad_recv.at[hour, step],
            rs_send.at[hour, step], rs_recv.at[hour, step], peer_id(step),
        )

    for g in range(GROUPS):
        for step in range(1, peers):
            ag_copy(g, step).start()

    region = region_ref[...]
    owner = lax.div(region, local)
    position = (
        lax.rem(owner, CORES) * half + lax.div(owner, CORES) * local + lax.rem(region, local)
    )
    slots = lax.broadcasted_iota(jnp.int32, (CORES * half, ev_count), 0)
    match[...] = jnp.where(slots == position, 1.0, 0.0).astype(jnp.bfloat16)

    node_cols = jnp.transpose(node_ref[0])

    def pick_rows(first, count, waits):
        lanes = lax.broadcasted_iota(jnp.int32, (ev_count, nodes), 1)
        for i in range(count):
            hit = node_cols[:, first + i : first + i + 1] == lanes
            picks[pl.ds(i * ev_count, ev_count), :] = jnp.where(hit, 1.0, 0.0).astype(jnp.bfloat16)

        def body(t, carry):
            if waits:
                pltpu.make_async_copy(
                    sens_hbm.at[0, :, pl.ds(0, tile)], sens.at[:, pl.ds(0, tile)], sens_sem.at[t]
                ).wait()
            cols = pl.ds(pl.multiple_of(t * tile, tile), tile)
            found = jnp.dot(
                picks[pl.ds(0, count * ev_count), :], sens[:, cols],
                preferred_element_type=jnp.float32,
            ).astype(jnp.bfloat16)
            for i in range(count):
                rows[first + i, :, cols] = found[i * ev_count : (i + 1) * ev_count]
            return carry

        lax.fori_loop(0, tiles, body, 0)

    def forward(g):
        def body(i, carry):
            hour = g * span + i
            table = gathered[hour].reshape(CORES * half, -1)
            looked = lax.dot_general(
                table, match[...], COLS_BY_COLS, preferred_element_type=jnp.float32
            )
            weighted = (power_ref[0, pl.ds(hour, 1), :] * looked).astype(jnp.bfloat16)
            for t in range(tiles):
                cols = pl.ds(t * tile, tile)
                part = jnp.dot(
                    weighted, rows[hour, :, cols], preferred_element_type=jnp.float32
                )
                volts[hour, :, cols] = part
                var_out[g, pl.ds(i, 1), cols] = jnp.sum(part * part, axis=0, keepdims=True)
            return carry

        lax.fori_loop(0, span, body, 0)
        for step in range(1, slices):
            var_copy(g, step).start()

    def backward(g):
        for step in range(1, slices):
            var_copy(g, step).wait_recv()
        variance = var_out[g]
        for step in range(1, slices):
            variance = variance + var_in[g, step]
        deviation = jnp.sqrt(variance + epsilon)
        margin = headroom_ref[0, pl.ds(g * span, span), :] - quantile * deviation
        margin_ref[0, pl.ds(g * span, span), :] = margin
        violation = jnp.maximum(-margin, 0.0)
        coef[pl.ds(g * span, span), :] = 2.0 * (quantile * violation / deviation)

        def body(i, carry):
            hour = g * span + i
            volt_grad = (coef[pl.ds(hour, 1), :] * volts[hour]).astype(jnp.bfloat16)
            weight_grad = lax.dot_general(
                volt_grad, rows[hour], ROWS_BY_ROWS, preferred_element_type=jnp.float32
            )
            load_grad = power_ref[0, pl.ds(hour, 1), :] * weight_grad
            high = load_grad.astype(jnp.bfloat16)
            low = (load_grad - high.astype(jnp.float32)).astype(jnp.bfloat16)
            total = lax.dot_general(
                match[...], high, ROWS_BY_ROWS, preferred_element_type=jnp.float32
            ) + lax.dot_general(
                match[...], low, ROWS_BY_ROWS, preferred_element_type=jnp.float32
            )
            grad[hour] = total.reshape(CORES, half, -1)
            rsc_copy(hour).start()
            return carry

        lax.fori_loop(0, span, body, 0)

    def reduce(g):
        def body(i, carry):
            hour = g * span + i
            rsc_copy(hour).wait_recv()
            total = grad[hour, core] + grad_in[hour]
            grad_in[hour] = total
            grad_out[hour] = total.astype(jnp.bfloat16)
            for step in range(1, peers):
                rs_copy(hour, step).start()
            return carry

        lax.fori_loop(0, span, body, 0)

    pick_rows(0, span, True)
    for step in range(1, peers):
        ag_copy(0, step).wait_recv()
    agc_copy(0).start()
    pick_rows(span, span // 2, False)
    agc_copy(0).wait_recv()
    forward(0)
    for step in range(1, peers):
        ag_copy(1, step).wait_recv()
    agc_copy(1).start()
    pick_rows(span + span // 2, span - span // 2, False)
    backward(0)
    agc_copy(1).wait_recv()
    forward(1)
    reduce(0)
    backward(1)
    reduce(1)

    for hour in range(hours):
        total = grad_in[hour, own, :]
        for step in range(1, peers):
            rs_copy(hour, step).wait_recv()
            total = total + grad_recv[hour, step].astype(jnp.float32)
        new_ref[:, hour, :] = load_ref[:, hour, :] - step_size * total

    for g in range(GROUPS):
        for step in range(1, peers):
            ag_copy(g, step).wait_send()
        agc_copy(g).wait_send()
        for step in range(1, slices):
            var_copy(g, step).wait_send()

    def drain(hour, carry):
        rsc_copy(hour).wait_send()
        for step in range(1, peers):
            rs_copy(hour, step).wait_send()
        return carry

    lax.fori_loop(0, hours, drain, 0)


def shards(sensitivity, headroom, ev_power, ev_node, region_map, loadings):
    nodes = sensitivity.shape[2]
    hours, ev_count = ev_power.shape[1:]
    local, _, columns = loadings.shape
    peers = lax.axis_size("feeder") // CORES
    slices = lax.axis_size("factor")
    half = peers * local
    span = hours // GROUPS
    tile = 256
    vmem = pl.BlockSpec(memory_space=pltpu.VMEM)
    dma = pltpu.SemaphoreType.DMA
    return pl.pallas_call(
        functools.partial(kernel, peers, slices, tile),
        out_shape=(
            jax.ShapeDtypeStruct(headroom.shape, jnp.float32),
            jax.ShapeDtypeStruct(loadings.shape, jnp.float32),
        ),
        in_specs=[pl.BlockSpec(memory_space=pl.ANY)] + [vmem] * 5,
        out_specs=(vmem, vmem),
        scratch_shapes=[
            pltpu.VMEM((nodes, nodes), jnp.bfloat16),
            pltpu.VMEM((span * ev_count, nodes), jnp.bfloat16),
            pltpu.VMEM((hours, ev_count, nodes), jnp.bfloat16),
            pltpu.VMEM((hours, columns, nodes), jnp.float32),
            pltpu.VMEM((CORES * half, ev_count), jnp.bfloat16),
            pltpu.VMEM((hours, CORES, half, columns), jnp.bfloat16),
            pltpu.VMEM((hours, nodes), jnp.float32),
            pltpu.VMEM((GROUPS, span, nodes), jnp.float32),
            pltpu.VMEM((GROUPS, slices, span, nodes), jnp.float32),
            pltpu.VMEM((hours, CORES, half, columns), jnp.float32),
            pltpu.VMEM((hours, half, columns), jnp.float32),
            pltpu.VMEM((hours, half, columns), jnp.bfloat16),
            pltpu.VMEM((hours, peers, local, columns), jnp.bfloat16),
            dma((nodes // tile,)),
            dma((GROUPS, peers)),
            dma((GROUPS, peers)),
            dma((GROUPS,)),
            dma((GROUPS,)),
            dma((GROUPS, slices)),
            dma((GROUPS, slices)),
            dma((hours,)),
            dma((hours,)),
            dma((hours, peers)),
            dma((hours, peers)),
        ],
        compiler_params=pltpu.CompilerParams(
            collective_id=0, has_side_effects=True, vmem_limit_bytes=60 * 1024 * 1024
        ),
    )(sensitivity, headroom, ev_power, ev_node, region_map, loadings)


def solution(mesh):
    return jax.shard_map(
        shards,
        mesh=mesh,
        in_specs=(
            P("feeder", None, None),
            P("feeder", None, None),
            P("feeder", None, None),
            P("feeder", None, None),
            P("feeder", None),
            P("feeder", None, "factor"),
        ),
        out_specs=(P("feeder", None, None), P("feeder", None, "factor")),
        check_vma=False,
    )
```

```python
import functools

import jax
import jax.numpy as jnp
from jax import lax
from jax.experimental import pallas as pl
from jax.experimental.pallas import tpu as pltpu
from jax.sharding import PartitionSpec as P

quantile = 1.645
epsilon = 1e-06
step_size = 16.0

CORES = 2
GROUPS = 4
HALVES = 2
MESH = pl.DeviceIdType.MESH
ROWS_BY_ROWS = (((1,), (1,)), ((), ()))
COLS_BY_COLS = (((0,), (0,)), ((), ()))


def kernel(
    peers, slices, tile, chunk,
    sens_hbm, headroom_ref, power_ref, node_ref, region_ref, load_ref,
    margin_ref, new_ref,
    sens, table, rows, volts, match, gathered, coef, var_out, var_in,
    grad, grad_in, grad_out, grad_recv,
    sens_sem, ag_send, ag_recv, agc_send, agc_recv, var_send, var_recv,
    rsc_send, rsc_recv, rs_send, rs_recv,
):
    hours, ev_count, nodes = rows.shape
    local = load_ref.shape[0]
    half = peers * local
    span = hours // GROUPS
    wide = hours // HALVES
    tiles = nodes // tile
    chunks = nodes // chunk
    feeder = lax.axis_index("feeder")
    factor = lax.axis_index("factor")
    core = lax.rem(feeder, CORES)
    place = lax.div(feeder, CORES)
    sibling = (place * CORES + (1 - core), factor)

    def peer(step):
        return lax.rem(place + step, peers)

    def peer_id(step):
        return (peer(step) * CORES + core, factor)

    def slice_id(step):
        return (feeder, lax.rem(factor + step, slices))

    def sens_copy(t):
        part = pl.ds(t * chunk, chunk)
        return pltpu.make_async_copy(
            sens_hbm.at[0, part, :], sens.at[part, :], sens_sem.at[t]
        )

    for t in range(chunks):
        sens_copy(t).start()

    barrier = pltpu.get_barrier_semaphore()
    for step in range(1, peers):
        pl.semaphore_signal(barrier, inc=1, device_id=peer_id(step), device_id_type=MESH)
    for step in range(1, slices):
        pl.semaphore_signal(barrier, inc=1, device_id=slice_id(step), device_id_type=MESH)
    pl.semaphore_signal(barrier, inc=1, device_id=sibling, device_id_type=MESH)

    own = pl.ds(pl.multiple_of(place * local, local), local)
    for hour in range(hours):
        gathered[hour, core, own, :] = load_ref[:, hour, :].astype(jnp.bfloat16)

    pl.semaphore_wait(barrier, peers + slices - 1)

    def remote(src, dst, send, recv, device):
        return pltpu.make_async_remote_copy(
            src_ref=src, dst_ref=dst, send_sem=send, recv_sem=recv,
            device_id=device, device_id_type=MESH,
        )

    def ag_copy(g, step):
        block = gathered.at[pl.ds(g * wide, wide), core, own, :]
        return remote(block, block, ag_send.at[g, step], ag_recv.at[g, step], peer_id(step))

    def agc_copy(g):
        block = gathered.at[pl.ds(g * wide, wide), core]
        return remote(block, block, agc_send.at[g], agc_recv.at[g], sibling)

    def var_copy(g, step):
        return remote(
            var_out.at[g], var_in.at[g, step], var_send.at[g, step], var_recv.at[g, step],
            slice_id(step),
        )

    def rsc_copy(hour):
        return remote(
            grad.at[hour, 1 - core], grad_in.at[hour], rsc_send.at[hour], rsc_recv.at[hour],
            sibling,
        )

    def rs_copy(hour, step):
        block = pl.ds(pl.multiple_of(peer(step) * local, local), local)
        return remote(
            grad_out.at[hour, block, :], grad_recv.at[hour, step],
            rs_send.at[hour, step], rs_recv.at[hour, step], peer_id(step),
        )

    for g in range(HALVES):
        for step in range(1, peers):
            ag_copy(g, step).start()

    region = region_ref[...]
    owner = lax.div(region, local)
    position = (
        lax.rem(owner, CORES) * half + lax.div(owner, CORES) * local + lax.rem(region, local)
    )
    slots = lax.broadcasted_iota(jnp.int32, (CORES * half, ev_count), 0)
    match[...] = jnp.where(slots == position, 1.0, 0.0).astype(jnp.bfloat16)

    def widen(t, carry):
        part = pl.ds(pl.multiple_of(t * chunk, chunk), chunk)
        pltpu.make_async_copy(
            sens_hbm.at[0, part, :], sens.at[part, :], sens_sem.at[t]
        ).wait()
        table[part, :] = sens[part, :].astype(jnp.float32)
        return carry

    lax.fori_loop(0, chunks, widen, 0)

    lines = lax.broadcasted_iota(jnp.int32, (8, nodes), 0)

    def pick_rows(first, count):
        blocks = ev_count // 16

        def body(step, carry):
            hour = first + lax.div(step, blocks)
            start = pl.multiple_of(lax.rem(step, blocks) * 16, 16)
            parts = []
            for part in range(2):
                found = jnp.zeros((8, nodes), jnp.float32)
                for line in range(8):
                    node = node_ref[0, hour, start + part * 8 + line]
                    found = jnp.where(lines == line, table[pl.ds(node, 1), :], found)
                parts.append(found)
            block = jnp.concatenate(parts, axis=0).astype(jnp.bfloat16)
            rows[hour, pl.ds(start, 16), :] = block
            return carry

        lax.fori_loop(0, count * blocks, body, 0)

    def forward(g):
        def body(i, carry):
            hour = g * span + i
            known = gathered[hour].reshape(CORES * half, -1)
            looked = lax.dot_general(
                known, match[...], COLS_BY_COLS, preferred_element_type=jnp.float32
            )
            weighted = (power_ref[0, pl.ds(hour, 1), :] * looked).astype(jnp.bfloat16)
            for t in range(tiles):
                cols = pl.ds(t * tile, tile)
                part = jnp.dot(
                    weighted, rows[hour, :, cols], preferred_element_type=jnp.float32
                )
                volts[hour, :, cols] = part
                var_out[g, pl.ds(i, 1), cols] = jnp.sum(part * part, axis=0, keepdims=True)
            return carry

        lax.fori_loop(0, span, body, 0)
        for step in range(1, slices):
            var_copy(g, step).start()

    def reduce(hour):
        rsc_copy(hour).wait_recv()
        total = grad[hour, core] + grad_in[hour]
        grad_in[hour] = total
        grad_out[hour] = total.astype(jnp.bfloat16)
        for step in range(1, peers):
            rs_copy(hour, step).start()

    def backward(g, late):
        for step in range(1, slices):
            var_copy(g, step).wait_recv()
        variance = var_out[g]
        for step in range(1, slices):
            variance = variance + var_in[g, step]
        deviation = jnp.sqrt(variance + epsilon)
        margin = headroom_ref[0, pl.ds(g * span, span), :] - quantile * deviation
        margin_ref[0, pl.ds(g * span, span), :] = margin
        violation = jnp.maximum(-margin, 0.0)
        coef[pl.ds(g * span, span), :] = 2.0 * (quantile * violation / deviation)

        def body(i, carry):
            hour = g * span + i
            volt_grad = (coef[pl.ds(hour, 1), :] * volts[hour]).astype(jnp.bfloat16)
            weight_grad = lax.dot_general(
                volt_grad, rows[hour], ROWS_BY_ROWS, preferred_element_type=jnp.float32
            )
            load_grad = power_ref[0, pl.ds(hour, 1), :] * weight_grad
            high = load_grad.astype(jnp.bfloat16)
            low = (load_grad - high.astype(jnp.float32)).astype(jnp.bfloat16)
            total = lax.dot_general(
                match[...], high, ROWS_BY_ROWS, preferred_element_type=jnp.float32
            ) + lax.dot_general(
                match[...], low, ROWS_BY_ROWS, preferred_element_type=jnp.float32
            )
            grad[hour] = total.reshape(CORES, half, -1)
            rsc_copy(hour).start()

            @pl.when(i >= late)
            def _():
                reduce(hour - 1)

            return carry

        lax.fori_loop(0, span, body, 0)

    pick_rows(0, wide)
    for step in range(1, peers):
        ag_copy(0, step).wait_recv()
    agc_copy(0).start()
    pick_rows(wide, span)
    agc_copy(0).wait_recv()
    forward(0)
    forward(1)
    for step in range(1, peers):
        ag_copy(1, step).wait_recv()
    agc_copy(1).start()
    pick_rows(wide + span, span)
    backward(0, 1)
    backward(1, 0)
    agc_copy(1).wait_recv()
    forward(2)
    reduce(wide - 1)
    forward(3)
    backward(2, 1)
    backward(3, 0)
    reduce(hours - 1)

    for hour in range(hours):
        total = grad_in[hour, own, :]
        for step in range(1, peers):
            rs_copy(hour, step).wait_recv()
            total = total + grad_recv[hour, step].astype(jnp.float32)
        new_ref[:, hour, :] = load_ref[:, hour, :] - step_size * total

    for g in range(HALVES):
        for step in range(1, peers):
            ag_copy(g, step).wait_send()
        agc_copy(g).wait_send()
    for g in range(GROUPS):
        for step in range(1, slices):
            var_copy(g, step).wait_send()

    def drain(hour, carry):
        rsc_copy(hour).wait_send()
        for step in range(1, peers):
            rs_copy(hour, step).wait_send()
        return carry

    lax.fori_loop(0, hours, drain, 0)


def hand_over(margin_ref, new_ref, margin_out, new_out, sem):
    margin_copy = pltpu.make_async_copy(margin_ref, margin_out, sem.at[0])
    new_copy = pltpu.make_async_copy(new_ref, new_out, sem.at[1])
    margin_copy.start()
    new_copy.start()
    margin_copy.wait()
    new_copy.wait()


def shards(sensitivity, headroom, ev_power, ev_node, region_map, loadings):
    nodes = sensitivity.shape[2]
    hours, ev_count = ev_power.shape[1:]
    local, _, columns = loadings.shape
    peers = lax.axis_size("feeder") // CORES
    slices = lax.axis_size("factor")
    half = peers * local
    span = hours // GROUPS
    tile = 256
    chunk = 256
    vmem = pl.BlockSpec(memory_space=pltpu.VMEM)
    dma = pltpu.SemaphoreType.DMA
    margin, new = pl.pallas_call(
        functools.partial(kernel, peers, slices, tile, chunk),
        out_shape=(
            jax.ShapeDtypeStruct(headroom.shape, jnp.float32),
            jax.ShapeDtypeStruct(loadings.shape, jnp.float32),
        ),
        in_specs=[
            pl.BlockSpec(memory_space=pl.ANY), vmem, vmem,
            pl.BlockSpec(memory_space=pltpu.SMEM), vmem, vmem,
        ],
        out_specs=(vmem, vmem),
        scratch_shapes=[
            pltpu.VMEM((nodes, nodes), jnp.bfloat16),
            pltpu.VMEM((nodes, nodes), jnp.float32),
            pltpu.VMEM((hours, ev_count, nodes), jnp.bfloat16),
            pltpu.VMEM((hours, columns, nodes), jnp.float32),
            pltpu.VMEM((CORES * half, ev_count), jnp.bfloat16),
            pltpu.VMEM((hours, CORES, half, columns), jnp.bfloat16),
            pltpu.VMEM((hours, nodes), jnp.float32),
            pltpu.VMEM((GROUPS, span, nodes), jnp.float32),
            pltpu.VMEM((GROUPS, slices, span, nodes), jnp.float32),
            pltpu.VMEM((hours, CORES, half, columns), jnp.float32),
            pltpu.VMEM((hours, half, columns), jnp.float32),
            pltpu.VMEM((hours, half, columns), jnp.bfloat16),
            pltpu.VMEM((hours, peers, local, columns), jnp.bfloat16),
            dma((nodes // chunk,)),
            dma((HALVES, peers)),
            dma((HALVES, peers)),
            dma((HALVES,)),
            dma((HALVES,)),
            dma((GROUPS, slices)),
            dma((GROUPS, slices)),
            dma((hours,)),
            dma((hours,)),
            dma((hours, peers)),
            dma((hours, peers)),
        ],
        compiler_params=pltpu.CompilerParams(
            collective_id=0, has_side_effects=True, vmem_limit_bytes=60 * 1024 * 1024
        ),
    )(sensitivity, headroom, ev_power, ev_node, region_map, loadings)
    whole = pl.BlockSpec(memory_space=pl.ANY)
    return pl.pallas_call(
        hand_over,
        out_shape=(
            jax.ShapeDtypeStruct(headroom.shape, jnp.float32),
            jax.ShapeDtypeStruct(loadings.shape, jnp.float32),
        ),
        in_specs=[whole, whole],
        out_specs=(whole, whole),
        scratch_shapes=[dma((2,))],
    )(margin, new)


def solution(mesh):
    return jax.shard_map(
        shards,
        mesh=mesh,
        in_specs=(
            P("feeder", None, None),
            P("feeder", None, None),
            P("feeder", None, None),
            P("feeder", None, None),
            P("feeder", None),
            P("feeder", None, "factor"),
        ),
        out_specs=(P("feeder", None, None), P("feeder", None, "factor")),
        check_vma=False,
    )
```

```python
import functools

import jax
import jax.numpy as jnp
from jax import lax
from jax.experimental import pallas as pl
from jax.experimental.pallas import tpu as pltpu
from jax.sharding import PartitionSpec as P

quantile = 1.645
epsilon = 1e-06
step_size = 16.0

CORES = 2
GROUPS = 4
HALVES = 2
LANES = 128
SLOTS = 4
MESH = pl.DeviceIdType.MESH
ROWS_BY_ROWS = (((1,), (1,)), ((), ()))
COLS_BY_COLS = (((0,), (0,)), ((), ()))


def kernel(
    peers, slices, tile, chunk,
    sens_hbm, headroom_ref, power_ref, node_ref, region_ref, load_ref,
    margin_ref, new_ref,
    sens, table, stage, rows, volts, match, gathered, coef, var_out, var_in,
    grad, grad_in, grad_out, grad_recv,
    sens_sem, ag_send, ag_recv, agc_send, agc_recv, var_send, var_recv,
    rsc_send, rsc_recv, rs_send, rs_recv,
):
    hours, ev_count, nodes = rows.shape
    local = load_ref.shape[0]
    half = peers * local
    span = hours // GROUPS
    wide = hours // HALVES
    tiles = nodes // tile
    chunks = nodes // chunk
    feeder = lax.axis_index("feeder")
    factor = lax.axis_index("factor")
    core = lax.rem(feeder, CORES)
    place = lax.div(feeder, CORES)
    sibling = (place * CORES + (1 - core), factor)

    def peer(step):
        return lax.rem(place + step, peers)

    def peer_id(step):
        return (peer(step) * CORES + core, factor)

    def slice_id(step):
        return (feeder, lax.rem(factor + step, slices))

    def sens_copy(t):
        slot = lax.rem(t, SLOTS)
        part = pl.ds(pl.multiple_of(t * chunk, chunk), chunk)
        return pltpu.make_async_copy(
            sens_hbm.at[0, part, :], sens.at[slot], sens_sem.at[slot]
        )

    for t in range(SLOTS):
        sens_copy(jnp.int32(t)).start()

    barrier = pltpu.get_barrier_semaphore()
    for step in range(1, peers):
        pl.semaphore_signal(barrier, inc=1, device_id=peer_id(step), device_id_type=MESH)
    for step in range(1, slices):
        pl.semaphore_signal(barrier, inc=1, device_id=slice_id(step), device_id_type=MESH)
    pl.semaphore_signal(barrier, inc=1, device_id=sibling, device_id_type=MESH)

    own = pl.ds(pl.multiple_of(place * local, local), local)
    for hour in range(hours):
        gathered[hour, core, own, :] = load_ref[:, hour, :].astype(jnp.bfloat16)

    pl.semaphore_wait(barrier, peers + slices - 1)

    def remote(src, dst, send, recv, device):
        return pltpu.make_async_remote_copy(
            src_ref=src, dst_ref=dst, send_sem=send, recv_sem=recv,
            device_id=device, device_id_type=MESH,
        )

    def ag_copy(g, step):
        block = gathered.at[pl.ds(g * wide, wide), core, own, :]
        return remote(block, block, ag_send.at[g, step], ag_recv.at[g, step], peer_id(step))

    def agc_copy(g):
        block = gathered.at[pl.ds(g * wide, wide), core]
        return remote(block, block, agc_send.at[g], agc_recv.at[g], sibling)

    def var_copy(g, step):
        return remote(
            var_out.at[g], var_in.at[g, step], var_send.at[g, step], var_recv.at[g, step],
            slice_id(step),
        )

    def rsc_copy(hour):
        return remote(
            grad.at[hour, 1 - core], grad_in.at[hour], rsc_send.at[hour], rsc_recv.at[hour],
            sibling,
        )

    def rs_copy(hour, step):
        block = pl.ds(pl.multiple_of(peer(step) * local, local), local)
        return remote(
            grad_out.at[hour, block, :], grad_recv.at[hour, step],
            rs_send.at[hour, step], rs_recv.at[hour, step], peer_id(step),
        )

    for step in range(1, peers):
        ag_copy(0, step).start()

    region = region_ref[...]
    owner = lax.div(region, local)
    position = (
        lax.rem(owner, CORES) * half + lax.div(owner, CORES) * local + lax.rem(region, local)
    )
    slots = lax.broadcasted_iota(jnp.int32, (CORES * half, ev_count), 0)
    match[...] = jnp.where(slots == position, 1.0, 0.0).astype(jnp.bfloat16)

    blocks = nodes // LANES
    pitch = blocks + 1

    def widen(t, carry):
        sens_copy(t).wait()
        wide_rows = sens[lax.rem(t, SLOTS)].astype(jnp.float32)
        for c in range(blocks):
            table[pl.ds(t * (chunk * pitch) + c, chunk, stride=pitch), :] = wide_rows[
                :, c * LANES : (c + 1) * LANES
            ]

        @pl.when(t + SLOTS < chunks)
        def _():
            sens_copy(t + SLOTS).start()

        return carry

    lax.fori_loop(0, chunks, widen, 0)

    stride = ev_count + 1

    def pick_rows(first, count):
        def hours_body(i, carry):
            hour = first + i

            def body(step, carry):
                for line in range(16):
                    load = step * 16 + line
                    node = node_ref[0, hour, load]
                    stage[pl.ds(load, blocks, stride=stride), :] = table[
                        pl.ds(node * pitch, blocks), :
                    ]
                return carry

            lax.fori_loop(0, ev_count // 16, body, 0)
            for c in range(blocks):
                rows[hour, :, c * LANES : (c + 1) * LANES] = stage[
                    pl.ds(c * stride, ev_count), :
                ].astype(jnp.bfloat16)
            return carry

        lax.fori_loop(0, count, hours_body, 0)

    def forward(g):
        def body(i, carry):
            hour = g * span + i
            known = gathered[hour].reshape(CORES * half, -1)
            looked = lax.dot_general(
                known, match[...], COLS_BY_COLS, preferred_element_type=jnp.float32
            )
            weighted = (power_ref[0, pl.ds(hour, 1), :] * looked).astype(jnp.bfloat16)
            for t in range(tiles):
                cols = pl.ds(t * tile, tile)
                part = jnp.dot(
                    weighted, rows[hour, :, cols], preferred_element_type=jnp.float32
                )
                volts[hour, :, cols] = part
                var_out[g, pl.ds(i, 1), cols] = jnp.sum(part * part, axis=0, keepdims=True)
            return carry

        lax.fori_loop(0, span, body, 0)
        for step in range(1, slices):
            var_copy(g, step).start()

    def reduce(hour):
        rsc_copy(hour).wait_recv()
        total = grad[hour, core] + grad_in[hour]
        grad_in[hour] = total
        grad_out[hour] = total.astype(jnp.bfloat16)
        for step in range(1, peers):
            rs_copy(hour, step).start()

    def backward(g, late):
        for step in range(1, slices):
            var_copy(g, step).wait_recv()
        variance = var_out[g]
        for step in range(1, slices):
            variance = variance + var_in[g, step]
        deviation = jnp.sqrt(variance + epsilon)
        margin = headroom_ref[0, pl.ds(g * span, span), :] - quantile * deviation
        margin_ref[0, pl.ds(g * span, span), :] = margin
        violation = jnp.maximum(-margin, 0.0)
        coef[pl.ds(g * span, span), :] = 2.0 * (quantile * violation / deviation)

        def body(i, carry):
            hour = g * span + i
            volt_grad = (coef[pl.ds(hour, 1), :] * volts[hour]).astype(jnp.bfloat16)
            weight_grad = lax.dot_general(
                volt_grad, rows[hour], ROWS_BY_ROWS, preferred_element_type=jnp.float32
            )
            load_grad = power_ref[0, pl.ds(hour, 1), :] * weight_grad
            high = load_grad.astype(jnp.bfloat16)
            low = (load_grad - high.astype(jnp.float32)).astype(jnp.bfloat16)
            total = lax.dot_general(
                match[...], high, ROWS_BY_ROWS, preferred_element_type=jnp.float32
            ) + lax.dot_general(
                match[...], low, ROWS_BY_ROWS, preferred_element_type=jnp.float32
            )
            grad[hour] = total.reshape(CORES, half, -1)
            rsc_copy(hour).start()

            @pl.when(i >= late)
            def _():
                reduce(hour - 1)

            return carry

        lax.fori_loop(0, span, body, 0)

    pick_rows(0, wide)
    for step in range(1, peers):
        ag_copy(0, step).wait_recv()
    agc_copy(0).start()
    for step in range(1, peers):
        ag_copy(1, step).start()
    pick_rows(wide, span)
    agc_copy(0).wait_recv()
    forward(0)
    forward(1)
    for step in range(1, peers):
        ag_copy(1, step).wait_recv()
    agc_copy(1).start()
    pick_rows(wide + span, span)
    backward(0, 1)
    backward(1, 0)
    agc_copy(1).wait_recv()
    forward(2)
    reduce(wide - 1)
    forward(3)
    backward(2, 1)
    backward(3, 0)
    reduce(hours - 1)

    for hour in range(hours):
        total = grad_in[hour, own, :]
        for step in range(1, peers):
            rs_copy(hour, step).wait_recv()
            total = total + grad_recv[hour, step].astype(jnp.float32)
        new_ref[:, hour, :] = load_ref[:, hour, :] - step_size * total

    for g in range(HALVES):
        for step in range(1, peers):
            ag_copy(g, step).wait_send()
        agc_copy(g).wait_send()
    for g in range(GROUPS):
        for step in range(1, slices):
            var_copy(g, step).wait_send()

    def drain(hour, carry):
        rsc_copy(hour).wait_send()
        for step in range(1, peers):
            rs_copy(hour, step).wait_send()
        return carry

    lax.fori_loop(0, hours, drain, 0)


def hand_over(margin_ref, new_ref, margin_out, new_out):
    margin_out[...] = margin_ref[...]
    new_out[...] = new_ref[...]


def shards(sensitivity, headroom, ev_power, ev_node, region_map, loadings):
    nodes = sensitivity.shape[2]
    hours, ev_count = ev_power.shape[1:]
    local, _, columns = loadings.shape
    peers = lax.axis_size("feeder") // CORES
    slices = lax.axis_size("factor")
    half = peers * local
    span = hours // GROUPS
    tile = 256
    chunk = 256
    vmem = pl.BlockSpec(memory_space=pltpu.VMEM)
    dma = pltpu.SemaphoreType.DMA
    margin, new = pl.pallas_call(
        functools.partial(kernel, peers, slices, tile, chunk),
        out_shape=(
            jax.ShapeDtypeStruct(headroom.shape, jnp.float32),
            jax.ShapeDtypeStruct(loadings.shape, jnp.float32),
        ),
        in_specs=[
            pl.BlockSpec(memory_space=pl.ANY), vmem, vmem,
            pl.BlockSpec(memory_space=pltpu.SMEM), vmem, vmem,
        ],
        out_specs=(vmem, vmem),
        scratch_shapes=[
            pltpu.VMEM((SLOTS, chunk, nodes), jnp.bfloat16),
            pltpu.VMEM(((nodes + 1) * (nodes // LANES + 1), LANES), jnp.float32),
            pltpu.VMEM(((nodes // LANES + 1) * (ev_count + 1), LANES), jnp.float32),
            pltpu.VMEM((hours, ev_count, nodes), jnp.bfloat16),
            pltpu.VMEM((hours, columns, nodes), jnp.float32),
            pltpu.VMEM((CORES * half, ev_count), jnp.bfloat16),
            pltpu.VMEM((hours, CORES, half, columns), jnp.bfloat16),
            pltpu.VMEM((hours, nodes), jnp.float32),
            pltpu.VMEM((GROUPS, span, nodes), jnp.float32),
            pltpu.VMEM((GROUPS, slices, span, nodes), jnp.float32),
            pltpu.VMEM((hours, CORES, half, columns), jnp.float32),
            pltpu.VMEM((hours, half, columns), jnp.float32),
            pltpu.VMEM((hours, half, columns), jnp.bfloat16),
            pltpu.VMEM((hours, peers, local, columns), jnp.bfloat16),
            dma((SLOTS,)),
            dma((HALVES, peers)),
            dma((HALVES, peers)),
            dma((HALVES,)),
            dma((HALVES,)),
            dma((GROUPS, slices)),
            dma((GROUPS, slices)),
            dma((hours,)),
            dma((hours,)),
            dma((hours, peers)),
            dma((hours, peers)),
        ],
        compiler_params=pltpu.CompilerParams(
            collective_id=0, has_side_effects=True, vmem_limit_bytes=60 * 1024 * 1024
        ),
    )(sensitivity, headroom, ev_power, ev_node, region_map, loadings)
    return pl.pallas_call(
        hand_over,
        out_shape=(
            jax.ShapeDtypeStruct(headroom.shape, jnp.float32),
            jax.ShapeDtypeStruct(loadings.shape, jnp.float32),
        ),
        in_specs=[vmem, vmem],
        out_specs=(vmem, vmem),
    )(margin, new)


def solution(mesh):
    return jax.shard_map(
        shards,
        mesh=mesh,
        in_specs=(
            P("feeder", None, None),
            P("feeder", None, None),
            P("feeder", None, None),
            P("feeder", None, None),
            P("feeder", None),
            P("feeder", None, "factor"),
        ),
        out_specs=(P("feeder", None, None), P("feeder", None, "factor")),
        check_vma=False,
    )
```

```python
import functools

import jax
import jax.numpy as jnp
from jax import lax
from jax.experimental import pallas as pl
from jax.experimental.pallas import tpu as pltpu
from jax.sharding import PartitionSpec as P

quantile = 1.645
epsilon = 1e-06
step_size = 16.0

CORES = 2
NEAR = 2
GROUPS = 4
HALVES = 2
LANES = 128
SLOTS = 4
MESH = pl.DeviceIdType.MESH
ROWS_BY_ROWS = (((1,), (1,)), ((), ()))
COLS_BY_COLS = (((0,), (0,)), ((), ()))


def kernel(
    peers, slices, tile, chunk,
    sens_hbm, headroom_ref, power_ref, node_ref, region_ref, load_ref,
    margin_ref, new_ref,
    sens, table, stage, rows, volts, match, gathered, coef, var_out, var_in,
    grad, grad_in, near_out, near_in, grad_out, grad_recv,
    sens_sem, ag_send, ag_recv, agn_send, agn_recv, agc_send, agc_recv,
    var_send, var_recv, rsc_send, rsc_recv, rsn_send, rsn_recv, rs_send, rs_recv,
):
    hours, ev_count, nodes = rows.shape
    local = load_ref.shape[0]
    far = peers // NEAR
    part_rows = far * local
    span = hours // GROUPS
    wide = hours // HALVES
    tiles = nodes // tile
    chunks = nodes // chunk
    feeder = lax.axis_index("feeder")
    factor = lax.axis_index("factor")
    core = lax.rem(feeder, CORES)
    place = lax.div(feeder, CORES)
    near = lax.rem(place, NEAR)
    outer = lax.div(place, NEAR)
    sibling = (place * CORES + (1 - core), factor)

    neighbour = ((outer * NEAR + 1 - near) * CORES + core, factor)

    def peer(step):
        return lax.rem(outer + step, far)

    def peer_id(step):
        return ((peer(step) * NEAR + near) * CORES + core, factor)

    def slice_id(step):
        return (feeder, lax.rem(factor + step, slices))

    def sens_copy(t):
        slot = lax.rem(t, SLOTS)
        part = pl.ds(pl.multiple_of(t * chunk, chunk), chunk)
        return pltpu.make_async_copy(
            sens_hbm.at[0, part, :], sens.at[slot], sens_sem.at[slot]
        )

    for t in range(SLOTS):
        sens_copy(jnp.int32(t)).start()

    barrier = pltpu.get_barrier_semaphore()
    for step in range(1, far):
        pl.semaphore_signal(barrier, inc=1, device_id=peer_id(step), device_id_type=MESH)
    for step in range(1, slices):
        pl.semaphore_signal(barrier, inc=1, device_id=slice_id(step), device_id_type=MESH)
    pl.semaphore_signal(barrier, inc=1, device_id=neighbour, device_id_type=MESH)
    pl.semaphore_signal(barrier, inc=1, device_id=sibling, device_id_type=MESH)

    own = pl.ds(pl.multiple_of(outer * local, local), local)
    for hour in range(hours):
        gathered[hour, core, near, own, :] = load_ref[:, hour, :].astype(jnp.bfloat16)

    pl.semaphore_wait(barrier, far + slices)

    def remote(src, dst, send, recv, device):
        return pltpu.make_async_remote_copy(
            src_ref=src, dst_ref=dst, send_sem=send, recv_sem=recv,
            device_id=device, device_id_type=MESH,
        )

    def ag_copy(g, step):
        block = gathered.at[pl.ds(g * wide, wide), core, near, own, :]
        return remote(block, block, ag_send.at[g, step], ag_recv.at[g, step], peer_id(step))

    def agn_copy(g):
        block = gathered.at[pl.ds(g * wide, wide), core, near]
        return remote(block, block, agn_send.at[g], agn_recv.at[g], neighbour)

    def agc_copy(g):
        block = gathered.at[pl.ds(g * wide, wide), core]
        return remote(block, block, agc_send.at[g], agc_recv.at[g], sibling)

    def var_copy(g, step):
        return remote(
            var_out.at[g], var_in.at[g, step], var_send.at[g, step], var_recv.at[g, step],
            slice_id(step),
        )

    def rsc_copy(g):
        group = pl.ds(g * span, span)
        return remote(
            grad.at[group, 1 - core], grad_in.at[group], rsc_send.at[g], rsc_recv.at[g], sibling
        )

    def rsn_copy(g):
        group = pl.ds(g * span, span)
        return remote(
            near_out.at[group], near_in.at[group], rsn_send.at[g], rsn_recv.at[g], neighbour
        )

    def rs_copy(g, step):
        group = pl.ds(g * span, span)
        return remote(
            grad_out.at[peer(step), group], grad_recv.at[step, group],
            rs_send.at[g, step], rs_recv.at[g, step], peer_id(step),
        )

    for step in range(1, far):
        ag_copy(0, step).start()

    region = region_ref[...]
    owner = lax.div(region, local)
    spot = lax.div(owner, CORES)
    position = (
        (lax.rem(owner, CORES) * NEAR + lax.rem(spot, NEAR)) * part_rows
        + lax.div(spot, NEAR) * local
        + lax.rem(region, local)
    )
    slots = lax.broadcasted_iota(jnp.int32, (CORES * NEAR * part_rows, ev_count), 0)
    match[...] = jnp.where(slots == position, 1.0, 0.0).astype(jnp.bfloat16)

    blocks = nodes // LANES
    pitch = blocks + 1

    def widen(t, carry):
        sens_copy(t).wait()
        wide_rows = sens[lax.rem(t, SLOTS)].astype(jnp.float32)
        for c in range(blocks):
            table[pl.ds(t * (chunk * pitch) + c, chunk, stride=pitch), :] = wide_rows[
                :, c * LANES : (c + 1) * LANES
            ]

        @pl.when(t + SLOTS < chunks)
        def _():
            sens_copy(t + SLOTS).start()

        return carry

    lax.fori_loop(0, chunks, widen, 0)

    stride = ev_count + 1

    def pick_rows(first, count):
        def hours_body(i, carry):
            hour = first + i

            def body(step, carry):
                for line in range(16):
                    load = step * 16 + line
                    node = node_ref[0, hour, load]
                    stage[pl.ds(load, blocks, stride=stride), :] = table[
                        pl.ds(node * pitch, blocks), :
                    ]
                return carry

            lax.fori_loop(0, ev_count // 16, body, 0)
            for c in range(blocks):
                rows[hour, :, c * LANES : (c + 1) * LANES] = stage[
                    pl.ds(c * stride, ev_count), :
                ].astype(jnp.bfloat16)
            return carry

        lax.fori_loop(0, count, hours_body, 0)

    def forward(g):
        for i in range(span):
            hour = g * span + i
            known = gathered[hour].reshape(CORES * NEAR * part_rows, -1)
            looked = lax.dot_general(
                known, match[...], COLS_BY_COLS, preferred_element_type=jnp.float32
            )
            weighted = (power_ref[0, hour : hour + 1, :] * looked).astype(jnp.bfloat16)
            for t in range(tiles):
                cols = pl.ds(t * tile, tile)
                part = jnp.dot(
                    weighted, rows[hour, :, cols], preferred_element_type=jnp.float32
                )
                volts[hour, :, cols] = part
                var_out[g, i : i + 1, cols] = jnp.sum(part * part, axis=0, keepdims=True)
        for step in range(1, slices):
            var_copy(g, step).start()

    def reduce_near(g):
        group = pl.ds(g * span, span)
        rsc_copy(g).wait_recv()
        near_out[group] = (grad[group, core, 1 - near] + grad_in[group, 1 - near]).astype(
            jnp.bfloat16
        )
        rsn_copy(g).start()

    def reduce_far(g):
        group = pl.ds(g * span, span)
        rsn_copy(g).wait_recv()
        total = (
            grad[group, core, near] + grad_in[group, near] + near_in[group].astype(jnp.float32)
        )
        grad_in[group, near] = total
        for block in range(far):
            grad_out[block, group] = total[:, block * local : (block + 1) * local].astype(
                jnp.bfloat16
            )
        for step in range(1, far):
            rs_copy(g, step).start()

    def backward(g):
        for step in range(1, slices):
            var_copy(g, step).wait_recv()
        variance = var_out[g]
        for step in range(1, slices):
            variance = variance + var_in[g, step]
        deviation = jnp.sqrt(variance + epsilon)
        margin = headroom_ref[0, pl.ds(g * span, span), :] - quantile * deviation
        margin_ref[0, pl.ds(g * span, span), :] = margin
        violation = jnp.maximum(-margin, 0.0)
        coef[pl.ds(g * span, span), :] = 2.0 * (quantile * violation / deviation)

        for i in range(span):
            hour = g * span + i
            volt_grad = (coef[hour : hour + 1, :] * volts[hour]).astype(jnp.bfloat16)
            weight_grad = lax.dot_general(
                volt_grad, rows[hour], ROWS_BY_ROWS, preferred_element_type=jnp.float32
            )
            load_grad = power_ref[0, hour : hour + 1, :] * weight_grad
            high = load_grad.astype(jnp.bfloat16)
            low = (load_grad - high.astype(jnp.float32)).astype(jnp.bfloat16)
            total = lax.dot_general(
                match[...], high, ROWS_BY_ROWS, preferred_element_type=jnp.float32
            ) + lax.dot_general(
                match[...], low, ROWS_BY_ROWS, preferred_element_type=jnp.float32
            )
            grad[hour] = total.reshape(CORES, NEAR, part_rows, -1)
        rsc_copy(g).start()

    def finish(g):
        for step in range(1, far):
            rs_copy(g, step).wait_recv()
        for hour in range(g * span, (g + 1) * span):
            total = grad_in[hour, near, own, :]
            for step in range(1, far):
                total = total + grad_recv[step, hour].astype(jnp.float32)
            new_ref[:, hour, :] = load_ref[:, hour, :] - step_size * total

    pick_rows(0, span)
    for step in range(1, far):
        ag_copy(0, step).wait_recv()
    agn_copy(0).start()
    for step in range(1, far):
        ag_copy(1, step).start()
    pick_rows(span, span)
    agn_copy(0).wait_recv()
    agc_copy(0).start()
    for step in range(1, far):
        ag_copy(1, step).wait_recv()
    agn_copy(1).start()
    pick_rows(wide, span)
    agc_copy(0).wait_recv()
    forward(0)
    agn_copy(1).wait_recv()
    agc_copy(1).start()
    forward(1)
    pick_rows(wide + span, span)
    backward(0)
    backward(1)
    reduce_near(0)
    agc_copy(1).wait_recv()
    forward(2)
    reduce_near(1)
    reduce_far(0)
    forward(3)
    reduce_far(1)
    backward(2)
    backward(3)
    reduce_near(2)
    finish(0)
    reduce_near(3)
    reduce_far(2)
    finish(1)
    reduce_far(3)
    finish(2)
    finish(3)

    for g in range(HALVES):
        for step in range(1, far):
            ag_copy(g, step).wait_send()
        agn_copy(g).wait_send()
        agc_copy(g).wait_send()
    for g in range(GROUPS):
        for step in range(1, slices):
            var_copy(g, step).wait_send()
        rsc_copy(g).wait_send()
        rsn_copy(g).wait_send()
        for step in range(1, far):
            rs_copy(g, step).wait_send()


def hand_over(margin_ref, new_ref, margin_out, new_out):
    margin_out[...] = margin_ref[...]
    new_out[...] = new_ref[...]


def shards(sensitivity, headroom, ev_power, ev_node, region_map, loadings):
    nodes = sensitivity.shape[2]
    hours, ev_count = ev_power.shape[1:]
    local, _, columns = loadings.shape
    peers = lax.axis_size("feeder") // CORES
    slices = lax.axis_size("factor")
    far = peers // NEAR
    part_rows = far * local
    span = hours // GROUPS
    tile = 256
    chunk = 256
    vmem = pl.BlockSpec(memory_space=pltpu.VMEM)
    dma = pltpu.SemaphoreType.DMA
    margin, new = pl.pallas_call(
        functools.partial(kernel, peers, slices, tile, chunk),
        out_shape=(
            jax.ShapeDtypeStruct(headroom.shape, jnp.float32),
            jax.ShapeDtypeStruct(loadings.shape, jnp.float32),
        ),
        in_specs=[
            pl.BlockSpec(memory_space=pl.ANY), vmem, vmem,
            pl.BlockSpec(memory_space=pltpu.SMEM), vmem, vmem,
        ],
        out_specs=(vmem, vmem),
        scratch_shapes=[
            pltpu.VMEM((SLOTS, chunk, nodes), jnp.bfloat16),
            pltpu.VMEM(((nodes + 1) * (nodes // LANES + 1), LANES), jnp.float32),
            pltpu.VMEM(((nodes // LANES + 1) * (ev_count + 1), LANES), jnp.float32),
            pltpu.VMEM((hours, ev_count, nodes), jnp.bfloat16),
            pltpu.VMEM((hours, columns, nodes), jnp.float32),
            pltpu.VMEM((CORES * NEAR * part_rows, ev_count), jnp.bfloat16),
            pltpu.VMEM((hours, CORES, NEAR, part_rows, columns), jnp.bfloat16),
            pltpu.VMEM((hours, nodes), jnp.float32),
            pltpu.VMEM((GROUPS, span, nodes), jnp.float32),
            pltpu.VMEM((GROUPS, slices, span, nodes), jnp.float32),
            pltpu.VMEM((hours, CORES, NEAR, part_rows, columns), jnp.float32),
            pltpu.VMEM((hours, NEAR, part_rows, columns), jnp.float32),
            pltpu.VMEM((hours, part_rows, columns), jnp.bfloat16),
            pltpu.VMEM((hours, part_rows, columns), jnp.bfloat16),
            pltpu.VMEM((far, hours, local, columns), jnp.bfloat16),
            pltpu.VMEM((far, hours, local, columns), jnp.bfloat16),
            dma((SLOTS,)),
            dma((HALVES, far)),
            dma((HALVES, far)),
            dma((HALVES,)),
            dma((HALVES,)),
            dma((HALVES,)),
            dma((HALVES,)),
            dma((GROUPS, slices)),
            dma((GROUPS, slices)),
            dma((GROUPS,)),
            dma((GROUPS,)),
            dma((GROUPS,)),
            dma((GROUPS,)),
            dma((GROUPS, far)),
            dma((GROUPS, far)),
        ],
        compiler_params=pltpu.CompilerParams(
            collective_id=0, has_side_effects=True, vmem_limit_bytes=60 * 1024 * 1024
        ),
    )(sensitivity, headroom, ev_power, ev_node, region_map, loadings)
    return pl.pallas_call(
        hand_over,
        out_shape=(
            jax.ShapeDtypeStruct(headroom.shape, jnp.float32),
            jax.ShapeDtypeStruct(loadings.shape, jnp.float32),
        ),
        in_specs=[vmem, vmem],
        out_specs=(vmem, vmem),
    )(margin, new)


def solution(mesh):
    return jax.shard_map(
        shards,
        mesh=mesh,
        in_specs=(
            P("feeder", None, None),
            P("feeder", None, None),
            P("feeder", None, None),
            P("feeder", None, None),
            P("feeder", None),
            P("feeder", None, "factor"),
        ),
        out_specs=(P("feeder", None, None), P("feeder", None, "factor")),
        check_vma=False,
    )
```

```python
import functools

import jax
import jax.numpy as jnp
from jax import lax
from jax.experimental import pallas as pl
from jax.experimental.pallas import tpu as pltpu
from jax.sharding import PartitionSpec as P

quantile = 1.645
epsilon = 1e-06
step_size = 16.0

CORES = 2
NEAR = 2
GROUPS = 4
HALVES = 2
LANES = 128
SLOTS = 4
MESH = pl.DeviceIdType.MESH
ROWS_BY_ROWS = (((1,), (1,)), ((), ()))
COLS_BY_COLS = (((0,), (0,)), ((), ()))


def kernel(
    peers, slices, tile, chunk,
    sens_hbm, headroom_ref, power_ref, node_ref, region_ref, load_ref,
    margin_ref, new_ref,
    sens, table, stage, rows, volts, match, gathered, var_out, var_in,
    grad, grad_in, near_out, near_in, grad_out, grad_recv,
    sens_sem, ag_send, ag_recv, agn_send, agn_recv, agc_send, agc_recv,
    var_send, var_recv, rsc_send, rsc_recv, rsn_send, rsn_recv, rs_send, rs_recv,
):
    hours, ev_count, nodes = rows.shape
    local = load_ref.shape[0]
    far = peers // NEAR
    part_rows = far * local
    span = hours // GROUPS
    wide = hours // HALVES
    tiles = nodes // tile
    chunks = nodes // chunk
    feeder = lax.axis_index("feeder")
    factor = lax.axis_index("factor")
    core = lax.rem(feeder, CORES)
    place = lax.div(feeder, CORES)
    near = lax.rem(place, NEAR)
    outer = lax.div(place, NEAR)
    sibling = (place * CORES + (1 - core), factor)

    neighbour = ((outer * NEAR + 1 - near) * CORES + core, factor)

    def peer(step):
        return lax.rem(outer + step, far)

    def peer_id(step):
        return ((peer(step) * NEAR + near) * CORES + core, factor)

    def slice_id(step):
        return (feeder, lax.rem(factor + step, slices))

    def sens_copy(t):
        slot = lax.rem(t, SLOTS)
        part = pl.ds(pl.multiple_of(t * chunk, chunk), chunk)
        return pltpu.make_async_copy(
            sens_hbm.at[0, part, :], sens.at[slot], sens_sem.at[slot]
        )

    for t in range(SLOTS):
        sens_copy(jnp.int32(t)).start()

    barrier = pltpu.get_barrier_semaphore()
    for step in range(1, far):
        pl.semaphore_signal(barrier, inc=1, device_id=peer_id(step), device_id_type=MESH)
    for step in range(1, slices):
        pl.semaphore_signal(barrier, inc=1, device_id=slice_id(step), device_id_type=MESH)
    pl.semaphore_signal(barrier, inc=1, device_id=neighbour, device_id_type=MESH)
    pl.semaphore_signal(barrier, inc=1, device_id=sibling, device_id_type=MESH)

    own = pl.ds(pl.multiple_of(outer * local, local), local)
    for hour in range(hours):
        gathered[hour, core, near, own, :] = load_ref[:, hour, :].astype(jnp.bfloat16)

    pl.semaphore_wait(barrier, far + slices)

    def remote(src, dst, send, recv, device):
        return pltpu.make_async_remote_copy(
            src_ref=src, dst_ref=dst, send_sem=send, recv_sem=recv,
            device_id=device, device_id_type=MESH,
        )

    def ag_copy(g, step):
        block = gathered.at[pl.ds(g * wide, wide), core, near, own, :]
        return remote(block, block, ag_send.at[g, step], ag_recv.at[g, step], peer_id(step))

    def agn_copy(g):
        block = gathered.at[pl.ds(g * wide, wide), core, near]
        return remote(block, block, agn_send.at[g], agn_recv.at[g], neighbour)

    def agc_copy(g):
        block = gathered.at[pl.ds(g * wide, wide), core]
        return remote(block, block, agc_send.at[g], agc_recv.at[g], sibling)

    def var_copy(g, step):
        return remote(
            var_out.at[g], var_in.at[g, step], var_send.at[g, step], var_recv.at[g, step],
            slice_id(step),
        )

    def rsc_copy(g):
        group = pl.ds(g * span, span)
        return remote(
            grad.at[group, 1 - core], grad_in.at[group], rsc_send.at[g], rsc_recv.at[g], sibling
        )

    def rsn_copy(g):
        group = pl.ds(g * span, span)
        return remote(
            near_out.at[group], near_in.at[group], rsn_send.at[g], rsn_recv.at[g], neighbour
        )

    def rs_copy(g, step):
        group = pl.ds(g * span, span)
        return remote(
            grad_out.at[peer(step), group], grad_recv.at[step, group],
            rs_send.at[g, step], rs_recv.at[g, step], peer_id(step),
        )

    for step in range(1, far):
        ag_copy(0, step).start()

    region = region_ref[...]
    owner = lax.div(region, local)
    spot = lax.div(owner, CORES)
    position = (
        (lax.rem(owner, CORES) * NEAR + lax.rem(spot, NEAR)) * part_rows
        + lax.div(spot, NEAR) * local
        + lax.rem(region, local)
    )
    slots = lax.broadcasted_iota(jnp.int32, (CORES * NEAR * part_rows, ev_count), 0)
    match[...] = jnp.where(slots == position, 1.0, 0.0).astype(jnp.bfloat16)

    blocks = nodes // LANES
    pitch = blocks + 1

    def widen(t, carry):
        sens_copy(t).wait()
        wide_rows = sens[lax.rem(t, SLOTS)].astype(jnp.float32)
        for c in range(blocks):
            table[pl.ds(t * (chunk * pitch) + c, chunk, stride=pitch), :] = wide_rows[
                :, c * LANES : (c + 1) * LANES
            ]

        @pl.when(t + SLOTS < chunks)
        def _():
            sens_copy(t + SLOTS).start()

        return carry

    lax.fori_loop(0, chunks, widen, 0)

    stride = ev_count + 1

    def pick_rows(hour):
        def body(step, carry):
            for line in range(16):
                load = step * 16 + line
                node = node_ref[0, hour, load]
                stage[pl.ds(load, blocks, stride=stride), :] = table[
                    pl.ds(node * pitch, blocks), :
                ]
            return carry

        lax.fori_loop(0, ev_count // 16, body, 0)
        for c in range(blocks):
            rows[hour, :, c * LANES : (c + 1) * LANES] = stage[
                pl.ds(c * stride, ev_count), :
            ].astype(jnp.bfloat16)

    def pick_step(hour, carry):
        pick_rows(hour)

        @pl.when(hour == span - 1)
        def _():
            for step in range(1, far):
                ag_copy(0, step).wait_recv()
            agn_copy(0).start()
            for step in range(1, far):
                ag_copy(1, step).start()

        @pl.when(hour == wide - 1)
        def _():
            agn_copy(0).wait_recv()
            agc_copy(0).start()

        @pl.when(hour == wide + span - 1)
        def _():
            for step in range(1, far):
                ag_copy(1, step).wait_recv()
            agn_copy(1).start()

        return carry

    def forward(g, carry):
        @pl.when(g == 0)
        def _():
            agc_copy(0).wait_recv()

        @pl.when(g == GROUPS // HALVES - 1)
        def _():
            agn_copy(1).wait_recv()
            agc_copy(1).start()

        @pl.when(g == GROUPS // HALVES)
        def _():
            agc_copy(1).wait_recv()

        def body(i, carry):
            hour = g * span + i
            known = gathered[hour].reshape(CORES * NEAR * part_rows, -1)
            looked = lax.dot_general(
                known, match[...], COLS_BY_COLS, preferred_element_type=jnp.float32
            )
            weighted = (power_ref[0, pl.ds(hour, 1), :] * looked).astype(jnp.bfloat16)
            for t in range(tiles):
                cols = pl.ds(t * tile, tile)
                part = jnp.dot(
                    weighted, rows[hour, :, cols], preferred_element_type=jnp.float32
                )
                volts[hour, :, cols] = part
                var_out[g, pl.ds(i, 1), cols] = jnp.sum(part * part, axis=0, keepdims=True)
            return carry

        lax.fori_loop(0, span, body, 0)
        for step in range(1, slices):
            var_copy(g, step).start()
        return carry

    def reduce_near(g):
        group = pl.ds(g * span, span)
        rsc_copy(g).wait_recv()
        near_out[group] = (grad[group, core, 1 - near] + grad_in[group, 1 - near]).astype(
            jnp.bfloat16
        )
        rsn_copy(g).start()

    def reduce_far(g):
        group = pl.ds(g * span, span)
        rsn_copy(g).wait_recv()
        total = (
            grad[group, core, near] + grad_in[group, near] + near_in[group].astype(jnp.float32)
        )
        grad_in[group, near] = total
        for block in range(far):
            grad_out[block, group] = total[:, block * local : (block + 1) * local].astype(
                jnp.bfloat16
            )
        for step in range(1, far):
            rs_copy(g, step).start()

    def backward(g):
        for step in range(1, slices):
            var_copy(g, step).wait_recv()

        def body(i, carry):
            hour = g * span + i
            variance = var_out[g, pl.ds(i, 1), :]
            for step in range(1, slices):
                variance = variance + var_in[g, step, pl.ds(i, 1), :]
            deviation = jnp.sqrt(variance + epsilon)
            margin = headroom_ref[0, pl.ds(hour, 1), :] - quantile * deviation
            margin_ref[0, pl.ds(hour, 1), :] = margin
            violation = jnp.maximum(-margin, 0.0)
            coef = 2.0 * (quantile * violation / deviation)
            volt_grad = (coef * volts[hour]).astype(jnp.bfloat16)
            weight_grad = lax.dot_general(
                volt_grad, rows[hour], ROWS_BY_ROWS, preferred_element_type=jnp.float32
            )
            load_grad = power_ref[0, pl.ds(hour, 1), :] * weight_grad
            high = load_grad.astype(jnp.bfloat16)
            low = (load_grad - high.astype(jnp.float32)).astype(jnp.bfloat16)
            total = lax.dot_general(
                match[...], high, ROWS_BY_ROWS, preferred_element_type=jnp.float32
            ) + lax.dot_general(
                match[...], low, ROWS_BY_ROWS, preferred_element_type=jnp.float32
            )
            grad[hour] = total.reshape(CORES, NEAR, part_rows, -1)
            return carry

        lax.fori_loop(0, span, body, 0)
        rsc_copy(g).start()

    def finish(g):
        for step in range(1, far):
            rs_copy(g, step).wait_recv()
        for i in range(span):
            hour = g * span + i
            total = grad_in[hour, near, own, :]
            for step in range(1, far):
                total = total + grad_recv[step, hour].astype(jnp.float32)
            new_ref[:, hour, :] = load_ref[:, hour, :] - step_size * total

    def turn(g, carry):
        @pl.when(g < GROUPS)
        def _():
            backward(g)

        @pl.when(jnp.logical_and(g >= 1, g <= GROUPS))
        def _():
            reduce_near(g - 1)

        @pl.when(jnp.logical_and(g >= 2, g <= GROUPS + 1))
        def _():
            reduce_far(g - 2)

        @pl.when(g >= 3)
        def _():
            finish(g - 3)

        return carry

    lax.fori_loop(0, hours, pick_step, 0)
    lax.fori_loop(0, GROUPS, forward, 0)
    lax.fori_loop(0, GROUPS + 3, turn, 0)

    for g in range(HALVES):
        for step in range(1, far):
            ag_copy(g, step).wait_send()
        agn_copy(g).wait_send()
        agc_copy(g).wait_send()
    for g in range(GROUPS):
        for step in range(1, slices):
            var_copy(g, step).wait_send()
        rsc_copy(g).wait_send()
        rsn_copy(g).wait_send()
        for step in range(1, far):
            rs_copy(g, step).wait_send()


def hand_over(margin_ref, new_ref, margin_out, new_out):
    margin_out[...] = margin_ref[...]
    new_out[...] = new_ref[...]


def shards(sensitivity, headroom, ev_power, ev_node, region_map, loadings):
    nodes = sensitivity.shape[2]
    hours, ev_count = ev_power.shape[1:]
    local, _, columns = loadings.shape
    peers = lax.axis_size("feeder") // CORES
    slices = lax.axis_size("factor")
    far = peers // NEAR
    part_rows = far * local
    span = hours // GROUPS
    tile = 256
    chunk = 256
    vmem = pl.BlockSpec(memory_space=pltpu.VMEM)
    dma = pltpu.SemaphoreType.DMA
    margin, new = pl.pallas_call(
        functools.partial(kernel, peers, slices, tile, chunk),
        out_shape=(
            jax.ShapeDtypeStruct(headroom.shape, jnp.float32),
            jax.ShapeDtypeStruct(loadings.shape, jnp.float32),
        ),
        in_specs=[
            pl.BlockSpec(memory_space=pl.ANY), vmem, vmem,
            pl.BlockSpec(memory_space=pltpu.SMEM), vmem, vmem,
        ],
        out_specs=(vmem, vmem),
        scratch_shapes=[
            pltpu.VMEM((SLOTS, chunk, nodes), jnp.bfloat16),
            pltpu.VMEM(((nodes + 1) * (nodes // LANES + 1), LANES), jnp.float32),
            pltpu.VMEM(((nodes // LANES + 1) * (ev_count + 1), LANES), jnp.float32),
            pltpu.VMEM((hours, ev_count, nodes), jnp.bfloat16),
            pltpu.VMEM((hours, columns, nodes), jnp.float32),
            pltpu.VMEM((CORES * NEAR * part_rows, ev_count), jnp.bfloat16),
            pltpu.VMEM((hours, CORES, NEAR, part_rows, columns), jnp.bfloat16),
            pltpu.VMEM((GROUPS, span, nodes), jnp.float32),
            pltpu.VMEM((GROUPS, slices, span, nodes), jnp.float32),
            pltpu.VMEM((hours, CORES, NEAR, part_rows, columns), jnp.float32),
            pltpu.VMEM((hours, NEAR, part_rows, columns), jnp.float32),
            pltpu.VMEM((hours, part_rows, columns), jnp.bfloat16),
            pltpu.VMEM((hours, part_rows, columns), jnp.bfloat16),
            pltpu.VMEM((far, hours, local, columns), jnp.bfloat16),
            pltpu.VMEM((far, hours, local, columns), jnp.bfloat16),
            dma((SLOTS,)),
            dma((HALVES, far)),
            dma((HALVES, far)),
            dma((HALVES,)),
            dma((HALVES,)),
            dma((HALVES,)),
            dma((HALVES,)),
            dma((GROUPS, slices)),
            dma((GROUPS, slices)),
            dma((GROUPS,)),
            dma((GROUPS,)),
            dma((GROUPS,)),
            dma((GROUPS,)),
            dma((GROUPS, far)),
            dma((GROUPS, far)),
        ],
        compiler_params=pltpu.CompilerParams(
            collective_id=0, has_side_effects=True, vmem_limit_bytes=60 * 1024 * 1024
        ),
    )(sensitivity, headroom, ev_power, ev_node, region_map, loadings)
    return pl.pallas_call(
        hand_over,
        out_shape=(
            jax.ShapeDtypeStruct(headroom.shape, jnp.float32),
            jax.ShapeDtypeStruct(loadings.shape, jnp.float32),
        ),
        in_specs=[vmem, vmem],
        out_specs=(vmem, vmem),
    )(margin, new)


def solution(mesh):
    return jax.shard_map(
        shards,
        mesh=mesh,
        in_specs=(
            P("feeder", None, None),
            P("feeder", None, None),
            P("feeder", None, None),
            P("feeder", None, None),
            P("feeder", None),
            P("feeder", None, "factor"),
        ),
        out_specs=(P("feeder", None, None), P("feeder", None, "factor")),
        check_vma=False,
    )
```

```python
import functools

import jax
import jax.numpy as jnp
from jax import lax
from jax.experimental import pallas as pl
from jax.experimental.pallas import tpu as pltpu
from jax.sharding import PartitionSpec as P

quantile = 1.645
epsilon = 1e-06
step_size = 16.0

CORES = 2
NEAR = 2
GROUPS = 4
HALVES = 2
LANES = 128
SLOTS = 4
MESH = pl.DeviceIdType.MESH
ROWS_BY_ROWS = (((1,), (1,)), ((), ()))
COLS_BY_COLS = (((0,), (0,)), ((), ()))


def kernel(
    peers, slices, tile, chunk,
    sens_hbm, headroom_ref, power_ref, node_ref, region_ref, load_ref,
    margin_ref, new_ref,
    sens, table, stage, rows, volts, match, gathered, var_out, var_in,
    grad, grad_in, near_out, near_in, grad_out, grad_recv,
    sens_sem, ag_send, ag_recv, agn_send, agn_recv, agc_send, agc_recv,
    var_send, var_recv, rsc_send, rsc_recv, rsn_send, rsn_recv, rs_send, rs_recv,
):
    hours, ev_count, nodes = rows.shape
    local = load_ref.shape[0]
    far = peers // NEAR
    part_rows = far * local
    span = hours // GROUPS
    wide = hours // HALVES
    tiles = nodes // tile
    chunks = nodes // chunk
    feeder = lax.axis_index("feeder")
    factor = lax.axis_index("factor")
    core = lax.rem(feeder, CORES)
    place = lax.div(feeder, CORES)
    near = lax.rem(place, NEAR)
    outer = lax.div(place, NEAR)
    sibling = (place * CORES + (1 - core), factor)

    neighbour = ((outer * NEAR + 1 - near) * CORES + core, factor)

    def peer(step):
        return lax.rem(outer + step, far)

    def peer_id(step):
        return ((peer(step) * NEAR + near) * CORES + core, factor)

    def slice_id(step):
        return (feeder, lax.rem(factor + step, slices))

    def sens_copy(t):
        slot = lax.rem(t, SLOTS)
        part = pl.ds(pl.multiple_of(t * chunk, chunk), chunk)
        return pltpu.make_async_copy(
            sens_hbm.at[0, part, :], sens.at[slot], sens_sem.at[slot]
        )

    for t in range(SLOTS):
        sens_copy(jnp.int32(t)).start()

    barrier = pltpu.get_barrier_semaphore()
    for step in range(1, far):
        pl.semaphore_signal(barrier, inc=1, device_id=peer_id(step), device_id_type=MESH)
    for step in range(1, slices):
        pl.semaphore_signal(barrier, inc=1, device_id=slice_id(step), device_id_type=MESH)
    pl.semaphore_signal(barrier, inc=1, device_id=neighbour, device_id_type=MESH)
    pl.semaphore_signal(barrier, inc=1, device_id=sibling, device_id_type=MESH)

    own = pl.ds(pl.multiple_of(outer * local, local), local)
    for hour in range(hours):
        gathered[hour, core, near, own, :] = load_ref[:, hour, :].astype(jnp.bfloat16)

    pl.semaphore_wait(barrier, far + slices)

    def remote(src, dst, send, recv, device):
        return pltpu.make_async_remote_copy(
            src_ref=src, dst_ref=dst, send_sem=send, recv_sem=recv,
            device_id=device, device_id_type=MESH,
        )

    def ag_copy(g, step):
        block = gathered.at[pl.ds(g * wide, wide), core, near, own, :]
        return remote(block, block, ag_send.at[g, step], ag_recv.at[g, step], peer_id(step))

    def agn_copy(g):
        block = gathered.at[pl.ds(g * wide, wide), core, near]
        return remote(block, block, agn_send.at[g], agn_recv.at[g], neighbour)

    def agc_copy(g):
        block = gathered.at[pl.ds(g * wide, wide), core]
        return remote(block, block, agc_send.at[g], agc_recv.at[g], sibling)

    def var_copy(g, step):
        return remote(
            var_out.at[g], var_in.at[g, step], var_send.at[g, step], var_recv.at[g, step],
            slice_id(step),
        )

    def rsc_copy(g):
        group = pl.ds(g * span, span)
        return remote(
            grad.at[group, 1 - core], grad_in.at[group], rsc_send.at[g], rsc_recv.at[g], sibling
        )

    def rsn_copy(g):
        group = pl.ds(g * span, span)
        return remote(
            near_out.at[group], near_in.at[group], rsn_send.at[g], rsn_recv.at[g], neighbour
        )

    def rs_copy(g, step):
        group = pl.ds(g * span, span)
        return remote(
            grad_out.at[peer(step), group], grad_recv.at[step, group],
            rs_send.at[g, step], rs_recv.at[g, step], peer_id(step),
        )

    for step in range(1, far):
        ag_copy(0, step).start()

    region = region_ref[...]
    owner = lax.div(region, local)
    spot = lax.div(owner, CORES)
    position = (
        (lax.rem(owner, CORES) * NEAR + lax.rem(spot, NEAR)) * part_rows
        + lax.div(spot, NEAR) * local
        + lax.rem(region, local)
    )
    slots = lax.broadcasted_iota(jnp.int32, (CORES * NEAR * part_rows, ev_count), 0)
    match[...] = jnp.where(slots == position, 1.0, 0.0).astype(jnp.bfloat16)

    blocks = nodes // LANES
    pitch = blocks + 1

    def widen(t, carry):
        sens_copy(t).wait()
        wide_rows = sens[lax.rem(t, SLOTS)].astype(jnp.float32)
        for c in range(blocks):
            table[pl.ds(t * (chunk * pitch) + c, chunk, stride=pitch), :] = wide_rows[
                :, c * LANES : (c + 1) * LANES
            ]

        @pl.when(t + SLOTS < chunks)
        def _():
            sens_copy(t + SLOTS).start()

        return carry

    lax.fori_loop(0, chunks, widen, 0)

    stride = ev_count + 1

    def pick_rows(hour):
        def body(step, carry):
            for line in range(16):
                load = step * 16 + line
                node = node_ref[0, hour, load]
                stage[pl.ds(load, blocks, stride=stride), :] = table[
                    pl.ds(node * pitch, blocks), :
                ]
            return carry

        lax.fori_loop(0, ev_count // 16, body, 0)
        for c in range(blocks):
            rows[hour, :, c * LANES : (c + 1) * LANES] = stage[
                pl.ds(c * stride, ev_count), :
            ].astype(jnp.bfloat16)

    def pick_step(hour, carry):
        pick_rows(hour)

        @pl.when(hour == span - 1)
        def _():
            for step in range(1, far):
                ag_copy(0, step).wait_recv()
            agn_copy(0).start()
            for step in range(1, far):
                ag_copy(1, step).start()

        @pl.when(hour == wide - 1)
        def _():
            agn_copy(0).wait_recv()
            agc_copy(0).start()

        @pl.when(hour == wide + span - 1)
        def _():
            for step in range(1, far):
                ag_copy(1, step).wait_recv()
            agn_copy(1).start()

        return carry

    def forward(g, carry):
        @pl.when(g == 0)
        def _():
            agc_copy(0).wait_recv()

        @pl.when(g == GROUPS // HALVES - 1)
        def _():
            agn_copy(1).wait_recv()
            agc_copy(1).start()

        @pl.when(g == GROUPS // HALVES)
        def _():
            agc_copy(1).wait_recv()

        def body(i, carry):
            hour = g * span + i
            known = gathered[hour].reshape(CORES * NEAR * part_rows, -1)
            looked = lax.dot_general(
                known, match[...], COLS_BY_COLS, preferred_element_type=jnp.float32
            )
            weighted = (power_ref[0, pl.ds(hour, 1), :] * looked).astype(jnp.bfloat16)
            for t in range(tiles):
                cols = pl.ds(t * tile, tile)
                part = jnp.dot(
                    weighted, rows[hour, :, cols], preferred_element_type=jnp.float32
                )
                volts[hour, :, cols] = part
                var_out[g, pl.ds(i, 1), cols] = jnp.sum(part * part, axis=0, keepdims=True)
            return carry

        lax.fori_loop(0, span, body, 0, unroll=True)
        for step in range(1, slices):
            var_copy(g, step).start()
        return carry

    def reduce_near(g):
        group = pl.ds(g * span, span)
        rsc_copy(g).wait_recv()
        near_out[group] = (grad[group, core, 1 - near] + grad_in[group, 1 - near]).astype(
            jnp.bfloat16
        )
        rsn_copy(g).start()

    def reduce_far(g):
        group = pl.ds(g * span, span)
        rsn_copy(g).wait_recv()
        total = (
            grad[group, core, near] + grad_in[group, near] + near_in[group].astype(jnp.float32)
        )
        grad_in[group, near] = total
        for block in range(far):
            grad_out[block, group] = total[:, block * local : (block + 1) * local].astype(
                jnp.bfloat16
            )
        for step in range(1, far):
            rs_copy(g, step).start()

    def backward(g):
        for step in range(1, slices):
            var_copy(g, step).wait_recv()

        def body(i, carry):
            hour = g * span + i
            variance = var_out[g, pl.ds(i, 1), :]
            for step in range(1, slices):
                variance = variance + var_in[g, step, pl.ds(i, 1), :]
            deviation = jnp.sqrt(variance + epsilon)
            margin = headroom_ref[0, pl.ds(hour, 1), :] - quantile * deviation
            margin_ref[0, pl.ds(hour, 1), :] = margin
            violation = jnp.maximum(-margin, 0.0)
            coef = 2.0 * (quantile * violation / deviation)
            volt_grad = (coef * volts[hour]).astype(jnp.bfloat16)
            weight_grad = lax.dot_general(
                volt_grad, rows[hour], ROWS_BY_ROWS, preferred_element_type=jnp.float32
            )
            load_grad = power_ref[0, pl.ds(hour, 1), :] * weight_grad
            total = lax.dot_general(
                match[...], load_grad.astype(jnp.bfloat16), ROWS_BY_ROWS,
                preferred_element_type=jnp.float32,
            )
            grad[hour] = total.reshape(CORES, NEAR, part_rows, -1)
            return carry

        lax.fori_loop(0, span, body, 0, unroll=True)
        rsc_copy(g).start()

    def finish(g):
        for step in range(1, far):
            rs_copy(g, step).wait_recv()
        for i in range(span):
            hour = g * span + i
            total = grad_in[hour, near, own, :]
            for step in range(1, far):
                total = total + grad_recv[step, hour].astype(jnp.float32)
            new_ref[:, hour, :] = load_ref[:, hour, :] - step_size * total

    def turn(g, carry):
        @pl.when(g < GROUPS)
        def _():
            backward(g)

        @pl.when(jnp.logical_and(g >= 1, g <= GROUPS))
        def _():
            reduce_near(g - 1)

        @pl.when(jnp.logical_and(g >= 2, g <= GROUPS + 1))
        def _():
            reduce_far(g - 2)

        @pl.when(g >= 3)
        def _():
            finish(g - 3)

        return carry

    lax.fori_loop(0, hours, pick_step, 0)
    lax.fori_loop(0, GROUPS, forward, 0)
    lax.fori_loop(0, GROUPS + 3, turn, 0)

    for g in range(HALVES):
        for step in range(1, far):
            ag_copy(g, step).wait_send()
        agn_copy(g).wait_send()
        agc_copy(g).wait_send()
    for g in range(GROUPS):
        for step in range(1, slices):
            var_copy(g, step).wait_send()
        rsc_copy(g).wait_send()
        rsn_copy(g).wait_send()
        for step in range(1, far):
            rs_copy(g, step).wait_send()


def hand_over(margin_ref, new_ref, margin_out, new_out):
    margin_out[...] = margin_ref[...]
    new_out[...] = new_ref[...]


def shards(sensitivity, headroom, ev_power, ev_node, region_map, loadings):
    nodes = sensitivity.shape[2]
    hours, ev_count = ev_power.shape[1:]
    local, _, columns = loadings.shape
    peers = lax.axis_size("feeder") // CORES
    slices = lax.axis_size("factor")
    far = peers // NEAR
    part_rows = far * local
    span = hours // GROUPS
    tile = 256
    chunk = 256
    vmem = pl.BlockSpec(memory_space=pltpu.VMEM)
    dma = pltpu.SemaphoreType.DMA
    margin, new = pl.pallas_call(
        functools.partial(kernel, peers, slices, tile, chunk),
        out_shape=(
            jax.ShapeDtypeStruct(headroom.shape, jnp.float32),
            jax.ShapeDtypeStruct(loadings.shape, jnp.float32),
        ),
        in_specs=[
            pl.BlockSpec(memory_space=pl.ANY), vmem, vmem,
            pl.BlockSpec(memory_space=pltpu.SMEM), vmem, vmem,
        ],
        out_specs=(vmem, vmem),
        scratch_shapes=[
            pltpu.VMEM((SLOTS, chunk, nodes), jnp.bfloat16),
            pltpu.VMEM(((nodes + 1) * (nodes // LANES + 1), LANES), jnp.float32),
            pltpu.VMEM(((nodes // LANES + 1) * (ev_count + 1), LANES), jnp.float32),
            pltpu.VMEM((hours, ev_count, nodes), jnp.bfloat16),
            pltpu.VMEM((hours, columns, nodes), jnp.float32),
            pltpu.VMEM((CORES * NEAR * part_rows, ev_count), jnp.bfloat16),
            pltpu.VMEM((hours, CORES, NEAR, part_rows, columns), jnp.bfloat16),
            pltpu.VMEM((GROUPS, span, nodes), jnp.float32),
            pltpu.VMEM((GROUPS, slices, span, nodes), jnp.float32),
            pltpu.VMEM((hours, CORES, NEAR, part_rows, columns), jnp.float32),
            pltpu.VMEM((hours, NEAR, part_rows, columns), jnp.float32),
            pltpu.VMEM((hours, part_rows, columns), jnp.bfloat16),
            pltpu.VMEM((hours, part_rows, columns), jnp.bfloat16),
            pltpu.VMEM((far, hours, local, columns), jnp.bfloat16),
            pltpu.VMEM((far, hours, local, columns), jnp.bfloat16),
            dma((SLOTS,)),
            dma((HALVES, far)),
            dma((HALVES, far)),
            dma((HALVES,)),
            dma((HALVES,)),
            dma((HALVES,)),
            dma((HALVES,)),
            dma((GROUPS, slices)),
            dma((GROUPS, slices)),
            dma((GROUPS,)),
            dma((GROUPS,)),
            dma((GROUPS,)),
            dma((GROUPS,)),
            dma((GROUPS, far)),
            dma((GROUPS, far)),
        ],
        compiler_params=pltpu.CompilerParams(
            collective_id=0, has_side_effects=True, vmem_limit_bytes=60 * 1024 * 1024
        ),
    )(sensitivity, headroom, ev_power, ev_node, region_map, loadings)
    return pl.pallas_call(
        hand_over,
        out_shape=(
            jax.ShapeDtypeStruct(headroom.shape, jnp.float32),
            jax.ShapeDtypeStruct(loadings.shape, jnp.float32),
        ),
        in_specs=[vmem, vmem],
        out_specs=(vmem, vmem),
    )(margin, new)


def solution(mesh):
    return jax.shard_map(
        shards,
        mesh=mesh,
        in_specs=(
            P("feeder", None, None),
            P("feeder", None, None),
            P("feeder", None, None),
            P("feeder", None, None),
            P("feeder", None),
            P("feeder", None, "factor"),
        ),
        out_specs=(P("feeder", None, None), P("feeder", None, "factor")),
        check_vma=False,
    )
```
